32 devices in a mesh: row: 4 (over x, core), col: 8 (over z, y).
Axes of the slice: x: 2, y: 2, z: 4, core: 2. Of those that a mesh axis runs over, the one named last changes fastest.
Arguments:
- features: bfloat16 [2048, 8, 128], P('row', 'col'), may hold values from -6 to 6
- first_weight: bfloat16 [128, 256], replicated, may hold values from -0.5 to 0.5
- first_bias: float32 [256], replicated, may hold values from -4 to 4
- second_weight: bfloat16 [256, 256], replicated, may hold values from -0.375 to 0.375
- second_bias: float32 [256], replicated, may hold values from -4 to 4
- tile_values: bfloat16 [128, 64, 128, 128], P('row', 'col'), may hold values from -0.09375 to 0.09375
- tile_columns: int32 [128, 64], P('row', 'col'), may hold values from 0 to 15
- tile_counts: int32 [128, 8], P('row', 'col'), may hold values from 1 to 8
Outputs:
- output: bfloat16 [16384, 256], P(('row', 'col'))
The draws below stay inside these ranges and needn't reach their ends.
Inputs may be any that keep to these rules, and one draw needn't show every extreme that they name: `tile_columns`: entries of slots at or beyond their block row's count are ignored.
All inputs are finite; a program needn't handle non-finite values.
Results may differ from the reference program's by a relative error of at most 0.015.
Values may be sent and summed in bfloat16 or wider, within the bound.
A program may use at most 128 MiB of HBM per device.

```python
import jax
import jax.numpy as jnp
from jax import lax

F = 128
H = 256
BLK = 128
SLOTS = 8
NODES = 16384
RBLK = 32
CBLK = 16
N_ROW = 4
N_COL = 8


def place_ends(values, own_key, low, largest):
    shape = values.shape
    place = [jax.random.randint(jax.random.fold_in(own_key, axis), (), 0, shape[axis]) for axis in range(len(shape))]
    values = values.at[tuple(place)].set(low)
    longest = shape.index(max(shape))
    place[longest] = (place[longest] + 1) % shape[longest]
    return values.at[tuple(place)].set(largest)


def level_of(key, dims, shards, least, largest):
    level, own = 1.0, jax.random.fold_in(key, 6)
    for dim, blocks in shards:
        draws = jnp.exp(jax.random.uniform(jax.random.fold_in(own, dim), (blocks,), jnp.float32, least / len(shards), largest / len(shards)))
        level = level * jnp.repeat(draws, dims[dim] // blocks).reshape([-1 if axis == dim else 1 for axis in range(len(dims))])
    return level


def gaussian(stream_key, shape, deviation, reach, pieces=(), held_as=jnp.bfloat16):
    array = deviation * jax.random.normal(stream_key, shape, jnp.float32)
    if pieces:
        array = array * level_of(stream_key, shape, pieces, -0.22, 0.18)
    return jnp.clip(array, -reach, reach).astype(held_as)


def setup_inputs(seed: int = 0) -> dict:
    keys = jax.random.split(jax.random.key(seed), 9)
    features = gaussian(keys[0], (NODES // N_COL, N_COL, F), 1.0, 6.0, ((0, 4), (1, 8)))
    first_weight = gaussian(keys[1], (F, H), F ** -0.5, 0.5)
    first_bias = gaussian(keys[2], (H,), 1.0, 4.0, (), jnp.float32)
    second_weight = gaussian(keys[3], (H, H), H ** -0.5, 0.375)
    second_bias = gaussian(keys[4], (H,), 1.0, 4.0, (), jnp.float32)
    tile_values = gaussian(keys[5], (N_ROW * RBLK, N_COL * SLOTS, BLK, BLK), (N_COL * SLOTS * BLK // 2) ** -0.5, 0.09375, ((0, 4), (1, 8)))
    tile_columns = place_ends(jax.random.randint(keys[6], (N_ROW * RBLK, N_COL * SLOTS), 0, CBLK), jax.random.fold_in(keys[6], 1), 0, CBLK - 1).astype(jnp.int32)
    tile_counts = place_ends(jax.random.randint(keys[7], (N_ROW * RBLK, N_COL), 1, SLOTS + 1), jax.random.fold_in(keys[7], 1), 1, SLOTS).astype(jnp.int32)
    return {"features": features, "first_weight": first_weight, "first_bias": first_bias, "second_weight": second_weight, "second_bias": second_bias, "tile_values": tile_values, "tile_columns": tile_columns, "tile_counts": tile_counts}


def aggregate(scaled, tile_values, tile_columns, tile_counts):
    hidden_width = scaled.shape[-1]
    zero_index = jnp.int32(0)

    def one_panel(row_index):
        row_start = (row_index * RBLK).astype(jnp.int32)

        def one_column(totals, col_index):
            column_rows = lax.dynamic_index_in_dim(scaled, col_index, 1, keepdims=False)
            column_rows = column_rows.reshape(CBLK, BLK, hidden_width)
            slot_start = (col_index * SLOTS).astype(jnp.int32)
            col_start = col_index.astype(jnp.int32)
            values = lax.dynamic_slice(tile_values, (row_start, slot_start, zero_index, zero_index), (RBLK, SLOTS, BLK, BLK))
            columns = lax.dynamic_slice(tile_columns, (row_start, slot_start), (RBLK, SLOTS))
            counts = lax.dynamic_slice(tile_counts, (row_start, col_start), (RBLK, 1))
            fetched = jnp.take(column_rows, columns, axis=0)
            usable = jnp.arange(SLOTS, dtype=jnp.int32)[None, :] < counts
            fetched = jnp.where(usable[:, :, None, None], fetched.astype(jnp.float32), jnp.float32(0.0))
            term = jnp.einsum("rsik,rskf->rif", values.astype(jnp.float32), fetched)
            term = lax.optimization_barrier(term.astype(jnp.bfloat16)).astype(jnp.float32)
            return totals + term, None

        start = jnp.zeros((RBLK, BLK, hidden_width), jnp.float32)
        totals, _ = lax.scan(one_column, start, jnp.arange(N_COL, dtype=jnp.int32))
        return totals.reshape(RBLK * BLK, hidden_width)

    summed = lax.map(one_panel, jnp.arange(N_ROW, dtype=jnp.int32))
    return summed.reshape(NODES, hidden_width)


def reference(features, first_weight, first_bias, second_weight, second_bias, tile_values, tile_columns, tile_counts):
    first = jnp.dot(features.reshape(NODES, F), first_weight, preferred_element_type=jnp.float32).astype(jnp.bfloat16)
    summed1 = aggregate(first.reshape(NODES // N_COL, N_COL, H), tile_values, tile_columns, tile_counts)
    hidden = jnp.maximum(summed1 + first_bias, 0.0).astype(jnp.bfloat16)
    second = jnp.dot(hidden, second_weight, preferred_element_type=jnp.float32).astype(jnp.bfloat16)
    summed2 = aggregate(second.reshape(NODES // N_COL, N_COL, H), tile_values, tile_columns, tile_counts)
    return jnp.maximum(summed2 + second_bias, 0.0).astype(jnp.bfloat16)
```

```python
import functools

import jax
import jax.numpy as jnp
from jax import lax
from jax.experimental import pallas as pl
from jax.experimental.pallas import tpu as pltpu
from jax.sharding import PartitionSpec as P

MESH = pl.DeviceIdType.MESH


def kernel(
    R, C, Y, Z, K,
    feat, w1, b1, w2, b2, cols, cnts, tiles_hbm, out,
    tiles, panel1, panel2, scr,
    send_a1, recv_a1, send_b1, recv_b1,
    send_a2, recv_a2, send_b2, recv_b2,
    tile_sem,
    g1s, g1r, a1s, a1r, c1s, c1r,
    g2s, g2r, a2s, a2r, c2s, c2r,
):
    RB, S, B, _ = tiles.shape
    NB = panel1.shape[0] - 1
    per_chunk = RB // K
    G = max(1, 16 * C // B)
    r = lax.axis_index("row")
    c = lax.axis_index("col")
    z, y = c // Y, c % Y

    def row_peer(d):
        return (lax.rem(r + d, R), c)

    def y_peer(d):
        return (r, z * Y + lax.rem(y + d, Y))

    def z_peer(d):
        return (r, lax.rem(z + d, Z) * Y + y)

    tile_copies = []
    for k in range(K):
        rows = pl.ds(k * per_chunk, per_chunk)
        tile_copies.append(pltpu.make_async_copy(tiles_hbm.at[rows], tiles.at[rows], tile_sem.at[k]))
    for copy in tile_copies:
        copy.start()

    barrier = pltpu.get_barrier_semaphore()
    for d in range(1, R):
        pl.semaphore_signal(barrier, inc=1, device_id=row_peer(d), device_id_type=MESH)
    for d in range(1, Y):
        pl.semaphore_signal(barrier, inc=1, device_id=y_peer(d), device_id_type=MESH)
    for d in range(1, Z):
        pl.semaphore_signal(barrier, inc=1, device_id=z_peer(d), device_id_type=MESH)
    pl.semaphore_wait(barrier, R + Y + Z - 3)

    def remote(src, dst, ss, rs, peer):
        return pltpu.make_async_remote_copy(
            src_ref=src, dst_ref=dst, send_sem=ss, recv_sem=rs, device_id=peer, device_id_type=MESH
        )

    own = pl.ds(r * K, K)
    gather1 = [
        remote(feat, panel1.at[own], g1s.at[d - 1], g1r.at[d - 1], row_peer(d)) for d in range(1, R)
    ]
    for copy in gather1:
        copy.start()
    panel1[own] = feat[...]
    panel1[NB] = jnp.zeros(panel1.shape[1:], panel1.dtype)
    panel2[NB] = jnp.zeros(panel2.shape[1:], panel2.dtype)
    for copy in gather1:
        copy.wait_recv()

    def product(i, panel):
        count = cnts[i, 0]
        left, right = [], []
        for s in range(S):
            j = jnp.where(s < count, cols[i, s], NB)
            left.append(tiles[i, s])
            right.append(panel[j])
        return jnp.dot(
            jnp.concatenate(left, axis=1), jnp.concatenate(right, axis=0), preferred_element_type=jnp.float32
        )

    def compute1(k):
        tile_copies[k].wait()

        def step(t, carry):
            for g in range(G):
                scr[g * B:(g + 1) * B, :] = product(k * per_chunk + t * G + g, panel1)
            for dest in range(C):
                piece = scr[pl.ds(dest, 16, stride=C), :]
                send_a1[k, dest % Y, dest // Y, pl.ds(pl.multiple_of(t * 16, 16), 16), :] = piece.astype(jnp.bfloat16)
            return carry

        lax.fori_loop(0, per_chunk // G, step, 0)

    def compute2(k):
        def step(dest, carry):
            send_a2[k, lax.rem(dest, Y), dest // Y] = product(dest * K + k, panel2).astype(jnp.bfloat16)
            return carry

        lax.fori_loop(0, C, step, 0)

    def finish1(k, total):
        hidden = jnp.dot(total.astype(jnp.bfloat16), w1[...], preferred_element_type=jnp.float32)
        hidden = jnp.maximum(hidden + b1[...], 0.0).astype(jnp.bfloat16)
        second = jnp.dot(hidden, w2[...], preferred_element_type=jnp.float32)
        panel2[r * K + k] = second.astype(jnp.bfloat16)
        copies = []
        for d in range(1, R):
            block = panel2.at[r * K + k]
            copy = remote(block, block, g2s.at[k, d - 1], g2r.at[k, d - 1], row_peer(d))
            copy.start()
            copies.append(copy)
        return copies

    def finish2(k, total):
        out[k * B:(k + 1) * B, :] = jnp.maximum(total + b2[...], 0.0).astype(jnp.bfloat16)
        return []

    def layer(compute, finish, send_a, recv_a, send_b, recv_b, sas, sar, scs, scr_sem):
        in_a, in_b, others = {}, {}, []

        def start_a(k):
            in_a[k] = [
                remote(
                    send_a.at[k, lax.rem(y + d, Y)], recv_a.at[k, d - 1],
                    sas.at[k, d - 1], sar.at[k, d - 1], y_peer(d),
                )
                for d in range(1, Y)
            ]
            for copy in in_a[k]:
                copy.start()

        def start_b(k):
            for copy in in_a[k]:
                copy.wait_recv()
            total = send_a[k, y].astype(jnp.float32)
            for d in range(1, Y):
                total = total + recv_a[k, d - 1].astype(jnp.float32)
            send_b[k] = total.astype(jnp.bfloat16)
            in_b[k] = [
                remote(
                    send_b.at[k, lax.rem(z + d, Z)], recv_b.at[k, d - 1],
                    scs.at[k, d - 1], scr_sem.at[k, d - 1], z_peer(d),
                )
                for d in range(1, Z)
            ]
            for copy in in_b[k]:
                copy.start()

        def end(k):
            for copy in in_b[k]:
                copy.wait_recv()
            total = send_b[k, z].astype(jnp.float32)
            for d in range(1, Z):
                total = total + recv_b[k, d - 1].astype(jnp.float32)
            others.extend(finish(k, total))

        for k in range(K + 2):
            if k < K:
                compute(k)
                start_a(k)
            if 1 <= k <= K:
                start_b(k - 1)
            if k >= 2:
                end(k - 2)
        return [x for k in range(K) for x in in_a[k] + in_b[k]], others

    sent1, gather2 = layer(
        compute1, finish1, send_a1, recv_a1, send_b1, recv_b1, a1s, a1r, c1s, c1r
    )
    for copy in gather2:
        copy.wait_recv()
    sent2, _ = layer(
        compute2, finish2, send_a2, recv_a2, send_b2, recv_b2, a2s, a2r, c2s, c2r
    )
    for copy in gather1 + sent1 + gather2 + sent2:
        copy.wait_send()


def local(R, C, features, first_weight, first_bias, second_weight, second_bias, tile_values, tile_columns, tile_counts):
    nodes_dev, _, F = features.shape
    H = first_weight.shape[1]
    RB, S, B, _ = tile_values.shape
    K = nodes_dev // B
    Z = 4 if C % 4 == 0 else 1
    Y = C // Z
    NB = R * K
    G = max(1, 16 * C // B)
    bf = jnp.bfloat16
    dma = pltpu.SemaphoreType.DMA
    vmem = pl.BlockSpec(memory_space=pltpu.VMEM)
    smem = pl.BlockSpec(memory_space=pltpu.SMEM)
    ya, za, ra = max(Y - 1, 1), max(Z - 1, 1), max(R - 1, 1)
    bufs = []
    for W in (F, H):
        bufs += [
            pltpu.VMEM((K, Y, Z, B, W), bf),
            pltpu.VMEM((K, ya, Z, B, W), bf),
            pltpu.VMEM((K, Z, B, W), bf),
            pltpu.VMEM((K, za, B, W), bf),
        ]
    return pl.pallas_call(
        functools.partial(kernel, R, C, Y, Z, K),
        out_shape=jax.ShapeDtypeStruct((nodes_dev, H), bf),
        in_specs=[vmem] * 5 + [smem] * 2 + [pl.BlockSpec(memory_space=pl.ANY)],
        out_specs=vmem,
        scratch_shapes=[
            pltpu.VMEM((RB, S, B, B), bf),
            pltpu.VMEM((NB + 1, B, F), bf),
            pltpu.VMEM((NB + 1, B, H), bf),
            pltpu.VMEM((G * B, F), jnp.float32),
            *bufs,
            dma((K,)),
            dma((ra,)), dma((ra,)),
            dma((K, ya)), dma((K, ya)), dma((K, za)), dma((K, za)),
            dma((K, ra)), dma((K, ra)),
            dma((K, ya)), dma((K, ya)), dma((K, za)), dma((K, za)),
        ],
        compiler_params=pltpu.CompilerParams(
            collective_id=0, has_side_effects=True, vmem_limit_bytes=56 * 1024 * 1024
        ),
    )(
        features.reshape(K, B, F), first_weight, first_bias.reshape(1, H), second_weight,
        second_bias.reshape(1, H), tile_columns, tile_counts, tile_values,
    )


def solution(mesh):
    return jax.shard_map(
        functools.partial(local, mesh.shape["row"], mesh.shape["col"]),
        mesh=mesh,
        in_specs=(
            P("row", "col", None), P(), P(), P(), P(),
            P("row", "col", None, None), P("row", "col"), P("row", "col"),
        ),
        out_specs=P(("row", "col"), None),
        check_vma=False,
    )
```

```python
import functools

import jax
import jax.numpy as jnp
from jax import lax
from jax.experimental import pallas as pl
from jax.experimental.pallas import tpu as pltpu
from jax.sharding import PartitionSpec as P

MESH = pl.DeviceIdType.MESH
CHUNK = 64
LAG_A, LAG_B = 2, 4
ORDER = (2, 1, 3, 0)


def kernel(
    R, C, Y, Z, K, KB,
    feat, w1, b1, w2, b2, cols_hbm, cnts_hbm, tiles_hbm, out,
    tiles, cols, cnts, panel1, panel2, scr,
    send_a1, recv_a1, send_b1, recv_b1,
    send_a2, recv_a2, send_b2, recv_b2,
    tile_sem, index_sem,
    x1s, x1r, f1s, f1r, o1s, o1r,
    a1s, a1r, c1s, c1r,
    g2s, g2r, a2s, a2r, c2s, c2r,
):
    RB, S, B, _ = tiles.shape
    NB = panel1.shape[0] - 1
    per_chunk = RB // K
    split = B // CHUNK
    G = max(1, 16 * C // B)
    X = R // 2
    r = lax.axis_index("row")
    c = lax.axis_index("col")
    z, y = c // Y, c % Y
    x, core = r // 2, r % 2

    def row_peer(d):
        return (lax.rem(r + d, R), c)

    def y_peer(d):
        return (r, z * Y + lax.rem(y + d, Y))

    def z_peer(d):
        return (r, lax.rem(z + d, Z) * Y + y)

    def x_peer(d):
        return (lax.rem(x + d, X) * 2 + core, c)

    core_peer = (x * 2 + 1 - core, c)

    index_copies = [
        pltpu.make_async_copy(cols_hbm, cols, index_sem.at[0]),
        pltpu.make_async_copy(cnts_hbm, cnts, index_sem.at[1]),
    ]
    for copy in index_copies:
        copy.start()

    def tile_copy(k):
        rows = pl.ds(k * per_chunk, per_chunk)
        return pltpu.make_async_copy(tiles_hbm.at[rows], tiles.at[rows], tile_sem.at[k])

    barrier = pltpu.get_barrier_semaphore()
    for d in range(1, R):
        pl.semaphore_signal(barrier, inc=1, device_id=row_peer(d), device_id_type=MESH)
    for d in range(1, Y):
        pl.semaphore_signal(barrier, inc=1, device_id=y_peer(d), device_id_type=MESH)
    for d in range(1, Z):
        pl.semaphore_signal(barrier, inc=1, device_id=z_peer(d), device_id_type=MESH)
    for k in range(K):
        tile_copy(k).start()
    pl.semaphore_wait(barrier, R + Y + Z - 3)

    def remote(src, dst, ss, rs, peer):
        return pltpu.make_async_remote_copy(
            src_ref=src, dst_ref=dst, send_sem=ss, recv_sem=rs, device_id=peer, device_id_type=MESH
        )

    def blocks1(owner, h):
        return panel1.at[pl.ds(owner * KB + h * (KB // 2), KB // 2)]

    halves = [feat.at[pl.ds(h * (KB // 2), KB // 2)] for h in range(2)]
    across = {
        (h, d): remote(halves[h], blocks1(r, h), x1s.at[h, d - 1], x1r.at[h, d - 1], x_peer(d))
        for h in range(2) for d in range(1, X)
    }
    beside = [remote(halves[h], blocks1(r, h), o1s.at[h], o1r.at[h], core_peer) for h in range(2)]
    for copy in list(across.values()) + beside:
        copy.start()
    panel1[pl.ds(r * KB, KB)] = feat[...]
    panel1[NB] = jnp.zeros(panel1.shape[1:], panel1.dtype)
    panel2[NB] = jnp.zeros(panel2.shape[1:], panel2.dtype)
    onward = []
    for (h, d), copy in across.items():
        copy.wait_recv()
        block = blocks1(lax.rem(x - d + X, X) * 2 + core, h)
        ahead = remote(block, block, f1s.at[h, d - 1], f1r.at[h, d - 1], core_peer)
        ahead.start()
        onward.append(ahead)
    for copy in beside + onward:
        copy.wait_recv()
    for copy in index_copies:
        copy.wait()

    def product(i, panel):
        count = cnts[0, i]
        left, right = [], []
        for s in range(S):
            j = jnp.where(s < count, cols[s, i], NB)
            left.append(tiles[i, s])
            right.append(panel[j])
        return jnp.dot(
            jnp.concatenate(left, axis=1), jnp.concatenate(right, axis=0), preferred_element_type=jnp.float32
        )

    class Sums:
        def __init__(self, bufs, sems, width):
            self.send_a, self.recv_a, self.send_b, self.recv_b = bufs
            self.sas, self.sar, self.sbs, self.sbr = sems
            self.width = width

        def copies_a(self, k, p):
            part = pl.ds(p * self.width, self.width)
            return [
                remote(
                    self.send_a.at[k, lax.rem(y + e, Y), part], self.recv_a.at[k, e - 1, part],
                    self.sas.at[k, p, e - 1], self.sar.at[k, p, e - 1], y_peer(e),
                )
                for e in range(1, Y)
            ]

        def copy_b(self, k, d):
            return remote(
                self.send_b.at[k, d - 1], self.recv_b.at[k, d - 1],
                self.sbs.at[k, d - 1], self.sbr.at[k, d - 1], z_peer(d),
            )

        def start_a(self, k, p):
            for copy in self.copies_a(k, p):
                copy.start()

        def pair_sum(self, k, d):
            total = self.send_a[k, y, d].astype(jnp.float32)
            for e in range(1, Y):
                total = total + self.recv_a[k, e - 1, d].astype(jnp.float32)
            return total

        def start_b(self, k, p):
            for copy in self.copies_a(k, p):
                copy.wait_recv()
            for d in ORDER:
                if d > 0 and d // self.width == p:
                    self.send_b[k, d - 1] = self.pair_sum(k, d).astype(jnp.bfloat16)
                    self.copy_b(k, d).start()

        def end(self, k):
            total = self.pair_sum(k, 0)
            for d in range(1, Z):
                self.copy_b(k, d).wait_recv()
                total = total + self.recv_b[k, d - 1].astype(jnp.float32)
            return total

        def wait_sends(self, k):
            for p in range(Z // self.width):
                for copy in self.copies_a(k, p):
                    copy.wait_send()
            for d in range(1, Z):
                self.copy_b(k, d).wait_send()

    sums1 = Sums((send_a1, recv_a1, send_b1, recv_b1), (a1s, a1r, c1s, c1r), Z)
    sums2 = Sums((send_a2, recv_a2, send_b2, recv_b2), (a2s, a2r, c2s, c2r), 1)

    def gather2(k):
        block = panel2.at[r * KB + k // split, pl.ds(pl.multiple_of(k % split * CHUNK, CHUNK), CHUNK)]
        return [remote(block, block, g2s.at[k, d - 1], g2r.at[k, d - 1], row_peer(d)) for d in range(1, R)]

    def layer1(k, carry):
        @pl.when(k < K)
        def _():
            tile_copy(k).wait()

            def step(t, inner):
                for g in range(G):
                    scr[g * B:(g + 1) * B, :] = product(k * per_chunk + t * G + g, panel1)
                for dest in range(C):
                    piece = scr[pl.ds(dest, 16, stride=C), :].astype(jnp.bfloat16)
                    d = lax.rem(dest // Y - z + Z, Z)
                    send_a1[k, dest % Y, d, pl.ds(pl.multiple_of(t * 16, 16), 16), :] = piece
                return inner

            lax.fori_loop(0, per_chunk // G, step, 0)
            sums1.start_a(k, 0)

        @pl.when((k >= LAG_A) & (k < K + LAG_A))
        def _():
            sums1.start_b(k - LAG_A, 0)

        @pl.when(k >= LAG_B)
        def _():
            n = k - LAG_B
            total = sums1.end(n).astype(jnp.bfloat16)
            hidden = jnp.dot(total, w1[...], preferred_element_type=jnp.float32)
            hidden = jnp.maximum(hidden + b1[...], 0.0).astype(jnp.bfloat16)
            second = jnp.dot(hidden, w2[...], preferred_element_type=jnp.float32).astype(jnp.bfloat16)
            panel2[r * KB + n // split, pl.ds(pl.multiple_of(n % split * CHUNK, CHUNK), CHUNK), :] = second
            for copy in gather2(n):
                copy.start()

        return carry

    lax.fori_loop(0, K + LAG_B, layer1, 0)

    def arrive(k, carry):
        for copy in gather2(k):
            copy.wait_recv()
        return carry

    lax.fori_loop(0, K, arrive, 0)

    def layer2(k, carry):
        for d in ORDER:
            if d >= Z:
                continue

            @pl.when(k < KB)
            def _():
                for e in list(range(1, Y)) + [0]:
                    to = lax.rem(y + e, Y)
                    dest = lax.rem(z + d, Z) * Y + to
                    send_a2[k, to, d] = product(dest * KB + k, panel2).astype(jnp.bfloat16)
                    if e == Y - 1:
                        sums2.start_a(k, d)

            @pl.when((k >= 1) & (k <= KB))
            def _():
                sums2.start_b(k - 1, d)

        @pl.when(k >= 2)
        def _():
            n = k - 2
            total = jnp.maximum(sums2.end(n) + b2[...], 0.0)
            out[pl.ds(pl.multiple_of(n * B, B), B), :] = total.astype(jnp.bfloat16)

        return carry

    lax.fori_loop(0, KB + 2, layer2, 0)

    for copy in list(across.values()) + beside + onward:
        copy.wait_send()

    def sent1(k, carry):
        sums1.wait_sends(k)
        for copy in gather2(k):
            copy.wait_send()
        return carry

    def sent2(k, carry):
        sums2.wait_sends(k)
        return carry

    lax.fori_loop(0, K, sent1, 0)
    lax.fori_loop(0, KB, sent2, 0)


def local(R, C, features, first_weight, first_bias, second_weight, second_bias, tile_values, tile_columns, tile_counts):
    nodes_dev, _, F = features.shape
    H = first_weight.shape[1]
    RB, S, B, _ = tile_values.shape
    K = nodes_dev // CHUNK
    KB = nodes_dev // B
    Z = 4
    Y = C // Z
    X = R // 2
    NB = R * KB
    G = max(1, 16 * C // B)
    bf = jnp.bfloat16
    dma = pltpu.SemaphoreType.DMA
    vmem = pl.BlockSpec(memory_space=pltpu.VMEM)
    hbm = pl.BlockSpec(memory_space=pl.ANY)
    bufs = []
    for n, rows, W in ((K, CHUNK, F), (KB, B, H)):
        bufs += [
            pltpu.VMEM((n, Y, Z, rows, W), bf),
            pltpu.VMEM((n, Y - 1, Z, rows, W), bf),
            pltpu.VMEM((n, Z - 1, rows, W), bf),
            pltpu.VMEM((n, Z - 1, rows, W), bf),
        ]
    return pl.pallas_call(
        functools.partial(kernel, R, C, Y, Z, K, KB),
        out_shape=jax.ShapeDtypeStruct((nodes_dev, H), bf),
        in_specs=[vmem] * 5 + [hbm] * 3,
        out_specs=vmem,
        scratch_shapes=[
            pltpu.VMEM((RB, S, B, B), bf),
            pltpu.SMEM((S, RB), jnp.int32),
            pltpu.SMEM((1, RB), jnp.int32),
            pltpu.VMEM((NB + 1, B, F), bf),
            pltpu.VMEM((NB + 1, B, H), bf),
            pltpu.VMEM((G * B, F), jnp.float32),
            *bufs,
            dma((K,)), dma((2,)),
            dma((2, X - 1)), dma((2, X - 1)), dma((2, X - 1)), dma((2, X - 1)), dma((2,)), dma((2,)),
            dma((K, 1, Y - 1)), dma((K, 1, Y - 1)), dma((K, Z - 1)), dma((K, Z - 1)),
            dma((K, R - 1)), dma((K, R - 1)),
            dma((KB, Z, Y - 1)), dma((KB, Z, Y - 1)), dma((KB, Z - 1)), dma((KB, Z - 1)),
        ],
        compiler_params=pltpu.CompilerParams(
            collective_id=0, has_side_effects=True, vmem_limit_bytes=56 * 1024 * 1024
        ),
    )(
        features.reshape(KB, B, F), first_weight, first_bias.reshape(1, H), second_weight,
        second_bias.reshape(1, H), tile_columns.T, tile_counts.T, tile_values,
    )


def solution(mesh):
    return jax.shard_map(
        functools.partial(local, mesh.shape["row"], mesh.shape["col"]),
        mesh=mesh,
        in_specs=(
            P("row", "col", None), P(), P(), P(), P(),
            P("row", "col", None, None), P("row", "col"), P("row", "col"),
        ),
        out_specs=P(("row", "col"), None),
        check_vma=False,
    )
```

```python
import functools

import jax
import jax.numpy as jnp
from jax import lax
from jax.experimental import pallas as pl
from jax.experimental.pallas import tpu as pltpu
from jax.sharding import PartitionSpec as P

MESH = pl.DeviceIdType.MESH
CHUNK = 64
LAG_A, LAG_B = 2, 3
ORDER = (2, 1, 3, 0)


def kernel(
    R, C, Y, Z, K, KB,
    feat, w1_hbm, b1_hbm, w2_hbm, b2_hbm, cols_hbm, cnts_hbm, tiles_hbm, out_hbm,
    w1, b1, w2, b2, out, tiles, cols, cnts, panel1, panel2, scr,
    send_a1, recv_a1, send_b1, recv_b1,
    send_a2, recv_a2, send_b2, recv_b2,
    tile_sem, local_sem, out_sem,
    x1s, x1r, f1s, f1r, o1s, o1r,
    a1s, a1r, c1s, c1r,
    g2s, g2r, f2s, f2r, a2s, a2r, c2s, c2r,
):
    RB, S, B, _ = tiles.shape
    NB = panel1.shape[0] - 1
    per_chunk = RB // K
    split = B // CHUNK
    G = max(1, 16 * C // B)
    X = R // 2
    r = lax.axis_index("row")
    c = lax.axis_index("col")
    z, y = c // Y, c % Y
    x, core = r // 2, r % 2

    def row_peer(d):
        return (lax.rem(r + d, R), c)

    def y_peer(d):
        return (r, z * Y + lax.rem(y + d, Y))

    def z_peer(d):
        return (r, lax.rem(z + d, Z) * Y + y)

    def x_peer(d):
        return (lax.rem(x + d, X) * 2 + core, c)

    core_peer = (x * 2 + 1 - core, c)

    def tile_copy(k):
        rows = pl.ds(k * per_chunk, per_chunk)
        return pltpu.make_async_copy(tiles_hbm.at[rows], tiles.at[rows], tile_sem.at[k])

    barrier = pltpu.get_barrier_semaphore()
    for d in range(1, R):
        pl.semaphore_signal(barrier, inc=1, device_id=row_peer(d), device_id_type=MESH)
    for d in range(1, Y):
        pl.semaphore_signal(barrier, inc=1, device_id=y_peer(d), device_id_type=MESH)
    for d in range(1, Z):
        pl.semaphore_signal(barrier, inc=1, device_id=z_peer(d), device_id_type=MESH)
    own = pl.ds(r * KB, KB)
    pairs = [
        (feat, panel1.at[own]), (cols_hbm, cols), (cnts_hbm, cnts),
        (w1_hbm, w1), (b1_hbm, b1), (w2_hbm, w2), (b2_hbm, b2),
    ]
    local_copies = [pltpu.make_async_copy(a, b, local_sem.at[n]) for n, (a, b) in enumerate(pairs)]
    for copy in local_copies:
        copy.start()
    for k in range(K):
        tile_copy(k).start()
    panel1[NB] = jnp.zeros(panel1.shape[1:], panel1.dtype)
    panel2[NB] = jnp.zeros(panel2.shape[1:], panel2.dtype)
    pl.semaphore_wait(barrier, R + Y + Z - 3)

    def remote(src, dst, ss, rs, peer):
        return pltpu.make_async_remote_copy(
            src_ref=src, dst_ref=dst, send_sem=ss, recv_sem=rs, device_id=peer, device_id_type=MESH
        )

    def blocks1(owner, h):
        return panel1.at[pl.ds(owner * KB + h * (KB // 2), KB // 2)]

    halves = [feat.at[pl.ds(h * (KB // 2), KB // 2)] for h in range(2)]
    across = {
        (h, d): remote(halves[h], blocks1(r, h), x1s.at[h, d - 1], x1r.at[h, d - 1], x_peer(d))
        for h in range(2) for d in range(1, X)
    }
    beside = [remote(halves[h], blocks1(r, h), o1s.at[h], o1r.at[h], core_peer) for h in range(2)]
    for copy in list(across.values()) + beside:
        copy.start()
    onward = []
    for (h, d), copy in across.items():
        copy.wait_recv()
        block = blocks1(lax.rem(x - d + X, X) * 2 + core, h)
        ahead = remote(block, block, f1s.at[h, d - 1], f1r.at[h, d - 1], core_peer)
        ahead.start()
        onward.append(ahead)
    for copy in beside + onward:
        copy.wait_recv()
    for copy in local_copies:
        copy.wait()

    def product(i, panel):
        count = cnts[0, i]
        left, right = [], []
        for s in range(S):
            j = jnp.where(s < count, cols[s, i], NB)
            left.append(tiles[i, s])
            right.append(panel[j])
        return jnp.dot(
            jnp.concatenate(left, axis=1), jnp.concatenate(right, axis=0), preferred_element_type=jnp.float32
        )

    class Sums:
        def __init__(self, bufs, sems, width):
            self.send_a, self.recv_a, self.send_b, self.recv_b = bufs
            self.sas, self.sar, self.sbs, self.sbr = sems
            self.width = width

        def copies_a(self, k, p):
            part = pl.ds(p * self.width, self.width)
            return [
                remote(
                    self.send_a.at[k, lax.rem(y + e, Y), part], self.recv_a.at[k, e - 1, part],
                    self.sas.at[k, p, e - 1], self.sar.at[k, p, e - 1], y_peer(e),
                )
                for e in range(1, Y)
            ]

        def copy_b(self, k, d):
            return remote(
                self.send_b.at[k, d - 1], self.recv_b.at[k, d - 1],
                self.sbs.at[k, d - 1], self.sbr.at[k, d - 1], z_peer(d),
            )

        def start_a(self, k, p):
            for copy in self.copies_a(k, p):
                copy.start()

        def pair_sum(self, k, d):
            total = self.send_a[k, y, d].astype(jnp.float32)
            for e in range(1, Y):
                total = total + self.recv_a[k, e - 1, d].astype(jnp.float32)
            return total

        def start_b(self, k, p):
            for copy in self.copies_a(k, p):
                copy.wait_recv()
            for d in ORDER:
                if d > 0 and d // self.width == p:
                    self.send_b[k, d - 1] = self.pair_sum(k, d).astype(jnp.bfloat16)
                    self.copy_b(k, d).start()

        def end(self, k):
            total = self.pair_sum(k, 0)
            for d in range(1, Z):
                self.copy_b(k, d).wait_recv()
                total = total + self.recv_b[k, d - 1].astype(jnp.float32)
            return total

        def wait_sends(self, k):
            for p in range(Z // self.width):
                for copy in self.copies_a(k, p):
                    copy.wait_send()
            for d in range(1, Z):
                self.copy_b(k, d).wait_send()

    sums1 = Sums((send_a1, recv_a1, send_b1, recv_b1), (a1s, a1r, c1s, c1r), Z)
    sums2 = Sums((send_a2, recv_a2, send_b2, recv_b2), (a2s, a2r, c2s, c2r), 1)

    def block2(owner, k):
        return panel2.at[owner * KB + k // split, pl.ds(pl.multiple_of(k % split * CHUNK, CHUNK), CHUNK)]

    def beside2(k):
        return [remote(block2(r, k), block2(r, k), g2s.at[k, 0], g2r.at[k, 0], core_peer)]

    def across2(k):
        block = block2(r, k)
        return [remote(block, block, g2s.at[k, d], g2r.at[k, d], x_peer(d)) for d in range(1, X)]

    def onward2(k):
        blocks = [block2(lax.rem(x - d + X, X) * 2 + core, k) for d in range(1, X)]
        return [
            remote(block, block, f2s.at[k, d], f2r.at[k, d], core_peer) for d, block in enumerate(blocks)
        ]

    def forward2(k):
        for copy in across2(k):
            copy.wait_recv()
        for copy in onward2(k):
            copy.start()

    def layer1(k, carry):
        @pl.when(k < K)
        def _():
            tile_copy(k).wait()

            def step(t, inner):
                for g in range(G):
                    scr[g * B:(g + 1) * B, :] = product(k * per_chunk + t * G + g, panel1)
                for dest in range(C):
                    piece = scr[pl.ds(dest, 16, stride=C), :].astype(jnp.bfloat16)
                    d = lax.rem(dest // Y - z + Z, Z)
                    send_a1[k, dest % Y, d, pl.ds(pl.multiple_of(t * 16, 16), 16), :] = piece
                return inner

            lax.fori_loop(0, per_chunk // G, step, 0)
            sums1.start_a(k, 0)

        @pl.when((k >= LAG_A) & (k < K + LAG_A))
        def _():
            sums1.start_b(k - LAG_A, 0)

        @pl.when(k >= LAG_B)
        def _():
            n = k - LAG_B
            total = sums1.end(n).astype(jnp.bfloat16)
            hidden = jnp.dot(total, w1[...], preferred_element_type=jnp.float32)
            hidden = jnp.maximum(hidden + b1[...], 0.0).astype(jnp.bfloat16)
            second = jnp.dot(hidden, w2[...], preferred_element_type=jnp.float32).astype(jnp.bfloat16)
            panel2[r * KB + n // split, pl.ds(pl.multiple_of(n % split * CHUNK, CHUNK), CHUNK), :] = second
            for copy in across2(n) + beside2(n):
                copy.start()

        @pl.when(k >= LAG_B + 1)
        def _():
            forward2(k - LAG_B - 1)

        return carry

    lax.fori_loop(0, K + LAG_B, layer1, 0)
    forward2(K - 1)

    def arrive(k, carry):
        for copy in beside2(k) + onward2(k):
            copy.wait_recv()
        return carry

    lax.fori_loop(0, K, arrive, 0)

    def out_copy(n):
        rows = pl.ds(pl.multiple_of(n * B, B), B)
        return pltpu.make_async_copy(out.at[rows], out_hbm.at[rows], out_sem.at[n])

    def layer2(k, carry):
        for d in ORDER:
            if d >= Z:
                continue

            @pl.when(k < KB)
            def _():
                for e in list(range(1, Y)) + [0]:
                    to = lax.rem(y + e, Y)
                    dest = lax.rem(z + d, Z) * Y + to
                    send_a2[k, to, d] = product(dest * KB + k, panel2).astype(jnp.bfloat16)
                    if e == Y - 1:
                        sums2.start_a(k, d)

            @pl.when((k >= 1) & (k <= KB))
            def _():
                sums2.start_b(k - 1, d)

        @pl.when(k >= 2)
        def _():
            n = k - 2
            total = jnp.maximum(sums2.end(n) + b2[...], 0.0)
            out[pl.ds(pl.multiple_of(n * B, B), B), :] = total.astype(jnp.bfloat16)
            out_copy(n).start()

        return carry

    lax.fori_loop(0, KB + 2, layer2, 0)

    for copy in list(across.values()) + beside + onward:
        copy.wait_send()

    def sent1(k, carry):
        sums1.wait_sends(k)
        for copy in across2(k) + beside2(k) + onward2(k):
            copy.wait_send()
        return carry

    def sent2(k, carry):
        sums2.wait_sends(k)
        out_copy(k).wait()
        return carry

    lax.fori_loop(0, K, sent1, 0)
    lax.fori_loop(0, KB, sent2, 0)


def local(R, C, features, first_weight, first_bias, second_weight, second_bias, tile_values, tile_columns, tile_counts):
    nodes_dev, _, F = features.shape
    H = first_weight.shape[1]
    RB, S, B, _ = tile_values.shape
    K = nodes_dev // CHUNK
    KB = nodes_dev // B
    Z = 4
    Y = C // Z
    X = R // 2
    NB = R * KB
    G = max(1, 16 * C // B)
    bf = jnp.bfloat16
    dma = pltpu.SemaphoreType.DMA
    hbm = pl.BlockSpec(memory_space=pl.ANY)
    bufs = []
    for n, rows, W in ((K, CHUNK, F), (KB, B, H)):
        bufs += [
            pltpu.VMEM((n, Y, Z, rows, W), bf),
            pltpu.VMEM((n, Y - 1, Z, rows, W), bf),
            pltpu.VMEM((n, Z - 1, rows, W), bf),
            pltpu.VMEM((n, Z - 1, rows, W), bf),
        ]
    return pl.pallas_call(
        functools.partial(kernel, R, C, Y, Z, K, KB),
        out_shape=jax.ShapeDtypeStruct((nodes_dev, H), bf),
        in_specs=[hbm] * 8,
        out_specs=hbm,
        scratch_shapes=[
            pltpu.VMEM((F, H), bf),
            pltpu.VMEM((1, H), jnp.float32),
            pltpu.VMEM((H, H), bf),
            pltpu.VMEM((1, H), jnp.float32),
            pltpu.VMEM((nodes_dev, H), bf),
            pltpu.VMEM((RB, S, B, B), bf),
            pltpu.SMEM((S, RB), jnp.int32),
            pltpu.SMEM((1, RB), jnp.int32),
            pltpu.VMEM((NB + 1, B, F), bf),
            pltpu.VMEM((NB + 1, B, H), bf),
            pltpu.VMEM((G * B, F), jnp.float32),
            *bufs,
            dma((K,)), dma((7,)), dma((KB,)),
            dma((2, X - 1)), dma((2, X - 1)), dma((2, X - 1)), dma((2, X - 1)), dma((2,)), dma((2,)),
            dma((K, 1, Y - 1)), dma((K, 1, Y - 1)), dma((K, Z - 1)), dma((K, Z - 1)),
            dma((K, X)), dma((K, X)), dma((K, X - 1)), dma((K, X - 1)),
            dma((KB, Z, Y - 1)), dma((KB, Z, Y - 1)), dma((KB, Z - 1)), dma((KB, Z - 1)),
        ],
        compiler_params=pltpu.CompilerParams(
            collective_id=0, has_side_effects=True, vmem_limit_bytes=56 * 1024 * 1024
        ),
    )(
        features.reshape(KB, B, F), first_weight, first_bias.reshape(1, H), second_weight,
        second_bias.reshape(1, H), tile_columns.T, tile_counts.T, tile_values,
    )


def solution(mesh):
    return jax.shard_map(
        functools.partial(local, mesh.shape["row"], mesh.shape["col"]),
        mesh=mesh,
        in_specs=(
            P("row", "col", None), P(), P(), P(), P(),
            P("row", "col", None, None), P("row", "col"), P("row", "col"),
        ),
        out_specs=P(("row", "col"), None),
        check_vma=False,
    )
```

```python
import functools

import jax
import jax.numpy as jnp
from jax import lax
from jax.experimental import pallas as pl
from jax.experimental.pallas import tpu as pltpu
from jax.sharding import PartitionSpec as P

MESH = pl.DeviceIdType.MESH
CHUNK = 64
LAG_A, LAG_B = 3, 6
ORDER = (2, 1, 3, 0)


def kernel(
    R, C, Y, Z, K, KB,
    feat, w1_hbm, b1_hbm, w2_hbm, b2_hbm, cols_hbm, cnts_hbm, tiles_hbm, out_hbm,
    w1, b1, w2, b2, out, tiles, cols, cnts, panel1, panel2, scr,
    send_a1, recv_a1, send_b1, recv_b1,
    send_a2, recv_a2, send_b2, recv_b2,
    tile_sem, local_sem, out_sem,
    x1s, x1r, f1s, f1r, o1s, o1r,
    a1s, a1r, c1s, c1r,
    g2s, g2r, f2s, f2r, a2s, a2r, c2s, c2r,
):
    RB, S, B, _ = tiles.shape
    NB = panel1.shape[0] - 1
    per_chunk = RB // K
    split = B // CHUNK
    G = max(1, 16 * C // B)
    X = R // 2
    r = lax.axis_index("row")
    c = lax.axis_index("col")
    z, y = c // Y, c % Y
    x, core = r // 2, r % 2

    def row_peer(d):
        return (lax.rem(r + d, R), c)

    def y_peer(d):
        return (r, z * Y + lax.rem(y + d, Y))

    def z_peer(d):
        return (r, lax.rem(z + d, Z) * Y + y)

    def x_peer(d):
        return (lax.rem(x + d, X) * 2 + core, c)

    core_peer = (x * 2 + 1 - core, c)

    def tile_copy(k):
        rows = pl.ds(k * per_chunk, per_chunk)
        return pltpu.make_async_copy(tiles_hbm.at[rows], tiles.at[rows], tile_sem.at[k])

    barrier = pltpu.get_barrier_semaphore()
    for d in range(1, R):
        pl.semaphore_signal(barrier, inc=1, device_id=row_peer(d), device_id_type=MESH)
    for d in range(1, Y):
        pl.semaphore_signal(barrier, inc=1, device_id=y_peer(d), device_id_type=MESH)
    for d in range(1, Z):
        pl.semaphore_signal(barrier, inc=1, device_id=z_peer(d), device_id_type=MESH)
    own = pl.ds(r * KB, KB)
    pairs = [
        (feat, panel1.at[own]), (cols_hbm, cols), (cnts_hbm, cnts),
        (w1_hbm, w1), (b1_hbm, b1), (w2_hbm, w2), (b2_hbm, b2),
    ]
    local_copies = [pltpu.make_async_copy(a, b, local_sem.at[n]) for n, (a, b) in enumerate(pairs)]
    for copy in local_copies:
        copy.start()
    panel1[NB] = jnp.zeros(panel1.shape[1:], panel1.dtype)
    panel2[NB] = jnp.zeros(panel2.shape[1:], panel2.dtype)
    pl.semaphore_wait(barrier, R + Y + Z - 3)

    def remote(src, dst, ss, rs, peer):
        return pltpu.make_async_remote_copy(
            src_ref=src, dst_ref=dst, send_sem=ss, recv_sem=rs, device_id=peer, device_id_type=MESH
        )

    def blocks1(owner, h):
        return panel1.at[pl.ds(owner * KB + h * (KB // 2), KB // 2)]

    halves = [feat.at[pl.ds(h * (KB // 2), KB // 2)] for h in range(2)]
    across = {
        (h, d): remote(halves[h], blocks1(r, h), x1s.at[h, d - 1], x1r.at[h, d - 1], x_peer(d))
        for h in range(2) for d in range(1, X)
    }
    beside = [remote(halves[h], blocks1(r, h), o1s.at[h], o1r.at[h], core_peer) for h in range(2)]
    for copy in list(across.values()) + beside:
        copy.start()
    for k in range(K):
        tile_copy(k).start()
    onward = []
    for (h, d), copy in across.items():
        copy.wait_recv()
        block = blocks1(lax.rem(x - d + X, X) * 2 + core, h)
        ahead = remote(block, block, f1s.at[h, d - 1], f1r.at[h, d - 1], core_peer)
        ahead.start()
        onward.append(ahead)
    for copy in beside + onward:
        copy.wait_recv()
    for copy in local_copies:
        copy.wait()

    def product(i, panel):
        count = cnts[0, i]
        left, right = [], []
        for s in range(S):
            j = jnp.where(s < count, cols[s, i], NB)
            left.append(tiles[i, s])
            right.append(panel[j])
        return jnp.dot(
            jnp.concatenate(left, axis=1), jnp.concatenate(right, axis=0), preferred_element_type=jnp.float32
        )

    class Sums:
        def __init__(self, bufs, sems, width):
            self.send_a, self.recv_a, self.send_b, self.recv_b = bufs
            self.sas, self.sar, self.sbs, self.sbr = sems
            self.width = width

        def copies_a(self, k, p):
            part = pl.ds(p * self.width, self.width)
            return [
                remote(
                    self.send_a.at[k, lax.rem(y + e, Y), part], self.recv_a.at[k, e - 1, part],
                    self.sas.at[k, p, e - 1], self.sar.at[k, p, e - 1], y_peer(e),
                )
                for e in range(1, Y)
            ]

        def copy_b(self, k, d):
            return remote(
                self.send_b.at[k, d - 1], self.recv_b.at[k, d - 1],
                self.sbs.at[k, d - 1], self.sbr.at[k, d - 1], z_peer(d),
            )

        def start_a(self, k, p):
            for copy in self.copies_a(k, p):
                copy.start()

        def pair_sum(self, k, d):
            total = self.send_a[k, y, d].astype(jnp.float32)
            for e in range(1, Y):
                total = total + self.recv_a[k, e - 1, d].astype(jnp.float32)
            return total

        def start_b(self, k, p):
            for copy in self.copies_a(k, p):
                copy.wait_recv()
            for d in ORDER:
                if d > 0 and d // self.width == p:
                    self.send_b[k, d - 1] = self.pair_sum(k, d).astype(jnp.bfloat16)
                    self.copy_b(k, d).start()

        def end(self, k):
            total = self.pair_sum(k, 0)
            for d in range(1, Z):
                self.copy_b(k, d).wait_recv()
                total = total + self.recv_b[k, d - 1].astype(jnp.float32)
            return total

        def wait_sends(self, k):
            for p in range(Z // self.width):
                for copy in self.copies_a(k, p):
                    copy.wait_send()
            for d in range(1, Z):
                self.copy_b(k, d).wait_send()

    sums1 = Sums((send_a1, recv_a1, send_b1, recv_b1), (a1s, a1r, c1s, c1r), Z)
    sums2 = Sums((send_a2, recv_a2, send_b2, recv_b2), (a2s, a2r, c2s, c2r), 1)

    def block2(owner, k):
        return panel2.at[owner * KB + k // split, pl.ds(pl.multiple_of(k % split * CHUNK, CHUNK), CHUNK)]

    def beside2(k):
        return [remote(block2(r, k), block2(r, k), g2s.at[k, 0], g2r.at[k, 0], core_peer)]

    def across2(k):
        block = block2(r, k)
        return [remote(block, block, g2s.at[k, d], g2r.at[k, d], x_peer(d)) for d in range(1, X)]

    def onward2(k):
        blocks = [block2(lax.rem(x - d + X, X) * 2 + core, k) for d in range(1, X)]
        return [
            remote(block, block, f2s.at[k, d], f2r.at[k, d], core_peer) for d, block in enumerate(blocks)
        ]

    def forward2(k):
        for copy in across2(k):
            copy.wait_recv()
        for copy in onward2(k):
            copy.start()

    def layer1(k, carry):
        @pl.when(k < K)
        def _():
            tile_copy(k).wait()

            def step(t, inner):
                for g in range(G):
                    scr[g * B:(g + 1) * B, :] = product(k * per_chunk + t * G + g, panel1)
                for dest in range(C):
                    piece = scr[pl.ds(dest, 16, stride=C), :].astype(jnp.bfloat16)
                    d = lax.rem(dest // Y - z + Z, Z)
                    send_a1[k, dest % Y, d, pl.ds(pl.multiple_of(t * 16, 16), 16), :] = piece
                return inner

            lax.fori_loop(0, per_chunk // G, step, 0)
            sums1.start_a(k, 0)

        @pl.when((k >= LAG_A) & (k < K + LAG_A))
        def _():
            sums1.start_b(k - LAG_A, 0)

        @pl.when(k >= LAG_B)
        def _():
            n = k - LAG_B
            total = sums1.end(n).astype(jnp.bfloat16)
            hidden = jnp.dot(total, w1[...], preferred_element_type=jnp.float32)
            hidden = jnp.maximum(hidden + b1[...], 0.0).astype(jnp.bfloat16)
            second = jnp.dot(hidden, w2[...], preferred_element_type=jnp.float32).astype(jnp.bfloat16)
            panel2[r * KB + n // split, pl.ds(pl.multiple_of(n % split * CHUNK, CHUNK), CHUNK), :] = second
            for copy in across2(n) + beside2(n):
                copy.start()


        return carry

    lax.fori_loop(0, K + LAG_B, layer1, 0)

    def forward(k, carry):
        forward2(k)
        return carry

    lax.fori_loop(0, K, forward, 0)

    def arrive(k, carry):
        for copy in beside2(k) + onward2(k):
            copy.wait_recv()
        return carry

    lax.fori_loop(0, K, arrive, 0)

    def out_copy(n):
        rows = pl.ds(pl.multiple_of(n * B, B), B)
        return pltpu.make_async_copy(out.at[rows], out_hbm.at[rows], out_sem.at[n])

    def layer2(k, carry):
        for d in ORDER:
            if d >= Z:
                continue

            @pl.when(k < KB)
            def _():
                for e in list(range(1, Y)) + [0]:
                    to = lax.rem(y + e, Y)
                    dest = lax.rem(z + d, Z) * Y + to
                    send_a2[k, to, d] = product(dest * KB + k, panel2).astype(jnp.bfloat16)
                    if e == Y - 1:
                        sums2.start_a(k, d)

            @pl.when((k >= 1) & (k <= KB))
            def _():
                sums2.start_b(k - 1, d)

        @pl.when(k >= 2)
        def _():
            n = k - 2
            total = jnp.maximum(sums2.end(n) + b2[...], 0.0)
            out[pl.ds(pl.multiple_of(n * B, B), B), :] = total.astype(jnp.bfloat16)
            out_copy(n).start()

        return carry

    lax.fori_loop(0, KB + 2, layer2, 0)

    for copy in list(across.values()) + beside + onward:
        copy.wait_send()

    def sent1(k, carry):
        sums1.wait_sends(k)
        for copy in across2(k) + beside2(k) + onward2(k):
            copy.wait_send()
        return carry

    def sent2(k, carry):
        sums2.wait_sends(k)
        out_copy(k).wait()
        return carry

    lax.fori_loop(0, K, sent1, 0)
    lax.fori_loop(0, KB, sent2, 0)


def local(R, C, features, first_weight, first_bias, second_weight, second_bias, tile_values, tile_columns, tile_counts):
    nodes_dev, _, F = features.shape
    H = first_weight.shape[1]
    RB, S, B, _ = tile_values.shape
    K = nodes_dev // CHUNK
    KB = nodes_dev // B
    Z = 4
    Y = C // Z
    X = R // 2
    NB = R * KB
    G = max(1, 16 * C // B)
    bf = jnp.bfloat16
    dma = pltpu.SemaphoreType.DMA
    hbm = pl.BlockSpec(memory_space=pl.ANY)
    bufs = []
    for n, rows, W in ((K, CHUNK, F), (KB, B, H)):
        bufs += [
            pltpu.VMEM((n, Y, Z, rows, W), bf),
            pltpu.VMEM((n, Y - 1, Z, rows, W), bf),
            pltpu.VMEM((n, Z - 1, rows, W), bf),
            pltpu.VMEM((n, Z - 1, rows, W), bf),
        ]
    return pl.pallas_call(
        functools.partial(kernel, R, C, Y, Z, K, KB),
        out_shape=jax.ShapeDtypeStruct((nodes_dev, H), bf),
        in_specs=[hbm] * 8,
        out_specs=hbm,
        scratch_shapes=[
            pltpu.VMEM((F, H), bf),
            pltpu.VMEM((1, H), jnp.float32),
            pltpu.VMEM((H, H), bf),
            pltpu.VMEM((1, H), jnp.float32),
            pltpu.VMEM((nodes_dev, H), bf),
            pltpu.VMEM((RB, S, B, B), bf),
            pltpu.SMEM((S, RB), jnp.int32),
            pltpu.SMEM((1, RB), jnp.int32),
            pltpu.VMEM((NB + 1, B, F), bf),
            pltpu.VMEM((NB + 1, B, H), bf),
            pltpu.VMEM((G * B, F), jnp.float32),
            *bufs,
            dma((K,)), dma((7,)), dma((KB,)),
            dma((2, X - 1)), dma((2, X - 1)), dma((2, X - 1)), dma((2, X - 1)), dma((2,)), dma((2,)),
            dma((K, 1, Y - 1)), dma((K, 1, Y - 1)), dma((K, Z - 1)), dma((K, Z - 1)),
            dma((K, X)), dma((K, X)), dma((K, X - 1)), dma((K, X - 1)),
            dma((KB, Z, Y - 1)), dma((KB, Z, Y - 1)), dma((KB, Z - 1)), dma((KB, Z - 1)),
        ],
        compiler_params=pltpu.CompilerParams(
            collective_id=0, has_side_effects=True, vmem_limit_bytes=56 * 1024 * 1024
        ),
    )(
        features.reshape(KB, B, F), first_weight, first_bias.reshape(1, H), second_weight,
        second_bias.reshape(1, H), tile_columns.T, tile_counts.T, tile_values,
    )


def solution(mesh):
    return jax.shard_map(
        functools.partial(local, mesh.shape["row"], mesh.shape["col"]),
        mesh=mesh,
        in_specs=(
            P("row", "col", None), P(), P(), P(), P(),
            P("row", "col", None, None), P("row", "col"), P("row", "col"),
        ),
        out_specs=P(("row", "col"), None),
        check_vma=False,
    )
```
